32 devices in a mesh: groups: 2 (over y), dp: 8 (over z, x), tensor: 2 (over core).
Axes of the slice: x: 2, y: 2, z: 4, core: 2. Of those that a mesh axis runs over, the one named last changes fastest.
Arguments:
- hidden_acts: bfloat16 [16, 128, 14336], P(('groups', 'dp'), None, 'tensor'), parts along dimension 0, may hold values from -6 to 6
- out_grads: bfloat16 [16, 128, 4096], P(('groups', 'dp'), None, 'tensor'), parts along dimension 0, may hold values from -6 to 6
- token_ids: int32 [16, 128], P(('groups', 'dp')), parts along dimension 0, may hold values from 0 to 128255, as said below
- proj_in: bfloat16 [64, 14336], P(None, 'tensor'), may hold values from -0.046875 to 0.046875
- proj_out: bfloat16 [64, 4096], P(None, 'tensor'), may hold values from -0.09375 to 0.09375
- test_feats: bfloat16 [1024, 4096], P('dp'), may hold values from -0.3984375 to 0.3984375
- resample_counts: int32 [16, 256], P(('groups', 'dp')), parts along dimension 0, may hold values from 0 to 2, as said below
Outputs:
- scores: float32 [16, 1024], P(('groups', 'dp')), parts along dimension 0
- boot_sums: float32 [512, 1024], P(('groups', 'dp')), parts along dimension 0
The draws below stay inside these ranges and needn't reach their ends.
There are 2 independent parts, one for each index of `groups`. The reference program is written for one: setup_inputs(seed, part) draws one part's arguments, and reference() takes and returns one part's arrays. A program takes and returns all parts, laid end to end along the dimension named above; an argument that names none is the same for every part. Nothing has to cross between parts.
Inputs may be any that keep to these rules, and one draw needn't show every extreme that they name: `token_ids`: each example is live from position 0 to its length and 0 after it; every example has at least 32 live tokens, which are never 0. `resample_counts`: for each resample b the counts over all examples sum to 8, and at least one example has count 2.
All inputs are finite; a program needn't handle non-finite values.
Results may differ from the reference program's by a relative error of at most 0.0029.
Values may be sent and summed in bfloat16 or wider, within the bound.
A program may use at most 64 MiB of HBM per device.

```python
from functools import partial
import jax
import jax.numpy as jnp
from jax import lax

D = 4096
FF = 14336
VOCAB = 128256
RANK = 64
LEN = 128
NTEST = 1024
BOOT = 256
EXAMPLES = 8


def draw_token_ids(key, part):
    key = jax.random.fold_in(key, 11)
    key_len, key_ids = jax.random.split(key)
    lengths = jax.random.randint(key_len, (EXAMPLES,), LEN // 4, LEN + 1)
    tokens = jax.random.randint(key_ids, (EXAMPLES, LEN), 1, VOCAB)
    position = jnp.arange(LEN)[None, :]
    return jnp.where(position < lengths[:, None], tokens, 0).astype(jnp.int32)


def draw_resample_counts(key, part):
    key = jax.random.fold_in(key, 23)
    key_many, key_perm = jax.random.split(key)
    doubled = jax.random.randint(key_many, (BOOT,), 1, EXAMPLES // 4 + 1)
    perm_keys = jax.random.split(key_perm, BOOT)
    places = jax.vmap(lambda one_key: jax.random.permutation(one_key, EXAMPLES))(perm_keys)
    limit = doubled[:, None]
    counts = jnp.where(places < limit, 2, jnp.where(places < 2 * limit, 0, 1))
    return counts.T.astype(jnp.int32)


def block_levels(rng, shape, shards, least, high):
    def one(axis_at, shards_of):
        heights = jax.random.uniform(jax.random.fold_in(jax.random.fold_in(rng, 6), axis_at), (shards_of,), jnp.float32, least / len(shards), high / len(shards))
        return jnp.repeat(jnp.exp(heights), shape[axis_at] // shards_of).reshape((-1,) + (1,) * (len(shape) - axis_at - 1))

    loudness = one(*shards[0])
    for cut in shards[1:]:
        loudness = loudness * one(*cut)
    return loudness


def centred(rng, dims, scale, bound, shards=(), kind=jnp.bfloat16):
    gain = block_levels(rng, dims, shards, -0.22, 0.18) if shards else 1.0
    result = jax.random.normal(rng, dims, jnp.float32) * scale * gain
    return jnp.minimum(jnp.maximum(result, -bound), bound).astype(kind)


def setup_inputs(seed: int = 0, part: int = 0) -> dict:
    arg_keys = jax.random.split(jax.random.key(seed), 8)
    part_keys = jax.random.split(jax.random.fold_in(arg_keys[7], part), 8)
    return {
        "hidden_acts": centred(part_keys[0], (EXAMPLES, LEN, FF), 1.0, 6.0, ((0, 8), (2, 2))),
        "out_grads": centred(part_keys[1], (EXAMPLES, LEN, D), 1.0, 6.0, ((0, 8), (2, 2))),
        "token_ids": draw_token_ids(jax.random.fold_in(jax.random.fold_in(arg_keys[7], part), 71), part),
        "proj_in": centred(arg_keys[3], (RANK, FF), FF ** -0.5, 0.046875, ((1, 2),)),
        "proj_out": centred(arg_keys[4], (RANK, D), D ** -0.5, 0.09375, ((1, 2),)),
        "test_feats": centred(arg_keys[5], (NTEST, RANK * RANK), 0.05, 0.3984375, ((0, 8),)),
        "resample_counts": draw_resample_counts(jax.random.fold_in(jax.random.fold_in(arg_keys[7], part), 71), part),
    }


def one_example(proj_in, proj_out, packed):
    acts, grads, ids = packed
    token_live = (ids != 0).astype(jnp.float32)
    live_count = jnp.sum(token_live)
    in_feat = lax.dot_general(proj_in, acts, (((1,), (1,)), ((), ())), preferred_element_type=jnp.float32)
    out_feat = lax.dot_general(proj_out, grads, (((1,), (1,)), ((), ())), preferred_element_type=jnp.float32)
    example_grad = jnp.dot(out_feat * token_live[None, :], in_feat.T, precision=lax.Precision.HIGHEST) / live_count
    return example_grad.reshape(-1).astype(jnp.bfloat16)


def reference(hidden_acts, out_grads, token_ids, proj_in, proj_out, test_feats, resample_counts):
    train_feats = lax.map(partial(one_example, proj_in, proj_out), (hidden_acts, out_grads, token_ids))
    scores = jnp.dot(train_feats, test_feats.T, preferred_element_type=jnp.float32)
    boot_sums = jnp.dot(resample_counts.astype(jnp.float32).T, scores, precision=lax.Precision.HIGHEST)
    return scores, boot_sums
```

```python
import functools

import jax
import jax.numpy as jnp
from jax import lax
from jax.experimental import pallas as pl
from jax.experimental.pallas import tpu as pltpu
from jax.sharding import PartitionSpec as P

MESH = pl.DeviceIdType.MESH
F32 = jnp.float32
NT = (((1,), (1,)), ((), ()))


def shards(hidden_acts, out_grads, token_ids, proj_in, proj_out, test_feats, resample_counts):
    token_live = (token_ids != 0).astype(jnp.float32)
    live_count = jnp.sum(token_live, axis=1)
    in_part = jnp.einsum("rf,elf->erl", proj_in, hidden_acts, preferred_element_type=jnp.float32)
    out_part = jnp.einsum("rd,eld->erl", proj_out, out_grads, preferred_element_type=jnp.float32)
    in_feat, out_feat = lax.psum((in_part, out_part), "tensor")
    example_grad = (
        jnp.einsum(
            "eol,eil->eoi",
            out_feat * token_live[:, None, :],
            in_feat,
            precision=lax.Precision.HIGHEST,
        )
        / live_count[:, None, None]
    )
    train_feats = example_grad.reshape(example_grad.shape[0], -1).astype(jnp.bfloat16)
    score_cols = lax.dot_general(
        lax.all_gather(train_feats, "dp", axis=0, tiled=True),
        test_feats,
        (((1,), (1,)), ((), ())),
        preferred_element_type=jnp.float32,
    )
    all_counts = lax.all_gather(resample_counts, "dp", axis=0, tiled=True).astype(jnp.float32)
    boot_cols = lax.dot_general(
        all_counts,
        score_cols,
        (((0,), (0,)), ((), ())),
        precision=lax.Precision.HIGHEST,
        preferred_element_type=jnp.float32,
    )
    score_local, boot_sums = (
        lax.all_to_all(score_cols, "dp", split_axis=0, concat_axis=1, tiled=True),
        lax.all_to_all(boot_cols, "dp", split_axis=0, concat_axis=1, tiled=True),
    )
    return (score_local, boot_sums)


def kernel(
    n, chunks,
    hid_hbm, grad_hbm, tok_hbm, pin_hbm, pout_hbm, test_hbm, cnt_hbm,
    score_ref, boot_ref,
    hid, grad, tok, pin, pout, test, cnt, part, other, feats, wide, every,
    load_sem, chunk_sem, pair_sem, cnt_send, cnt_recv, feat_send, feat_recv, sc_send, sc_recv,
):
    me = lax.axis_index("dp")
    core = lax.axis_index("tensor")
    rank = pout.shape[0]
    half = rank // 2
    tests = test.shape[0]
    boots = boot_ref.shape[0]
    peers = [lax.rem(me + k, n) for k in range(1, n)]
    froms = [lax.rem(me + n - k, n) for k in range(1, n)]

    barrier = pltpu.get_barrier_semaphore()
    pl.semaphore_signal(barrier, inc=1, device_id={"tensor": 1 - core}, device_id_type=MESH)
    for peer in peers:
        pl.semaphore_signal(barrier, inc=1, device_id={"dp": peer}, device_id_type=MESH)

    def load(src, dst, sem):
        copy = pltpu.make_async_copy(src, dst, sem)
        copy.start()
        return copy

    load_pout = load(pout_hbm, pout, load_sem.at[0])
    load_grad = load(grad_hbm.at[0], grad, load_sem.at[1])
    width = hid.shape[1] // chunks
    loads = []
    for c in range(chunks):
        cols = pl.ds(c * width, width)
        loads.append((
            load(pin_hbm.at[:, cols], pin.at[:, cols], chunk_sem.at[0, c]),
            load(hid_hbm.at[0, :, cols], hid.at[:, cols], chunk_sem.at[1, c]),
        ))
    mine = pl.ds(me, 1)
    load_cnt = load(cnt_hbm, cnt.at[mine, :], load_sem.at[2])
    load_tok = load(tok_hbm, tok, load_sem.at[3])
    load_test = load(test_hbm, test, load_sem.at[4])

    load_pout.wait()
    load_grad.wait()
    part[0:rank, :] = lax.dot_general(pout[...], grad[...], NT, preferred_element_type=F32)
    total = None
    for c in range(chunks):
        for copy in loads[c]:
            copy.wait()
        cols = slice(c * width, (c + 1) * width)
        term = lax.dot_general(pin[:, cols], hid[:, cols], NT, preferred_element_type=F32)
        total = term if total is None else total + term
    part[rank:, :] = total

    pl.semaphore_wait(barrier, n)
    pair = pltpu.make_async_remote_copy(
        src_ref=part, dst_ref=other, send_sem=pair_sem.at[0], recv_sem=pair_sem.at[1],
        device_id={"tensor": 1 - core}, device_id_type=MESH,
    )
    pair.start()

    load_cnt.wait()
    sends = []

    def to_all(ref, send_sem, recv_sem):
        for k, peer in enumerate(peers):
            copy = pltpu.make_async_remote_copy(
                src_ref=ref, dst_ref=ref, send_sem=send_sem.at[k], recv_sem=recv_sem.at[k],
                device_id={"dp": peer}, device_id_type=MESH,
            )
            copy.start()
            sends.append(copy)

    def arrived(ref, k, send_sem, recv_sem):
        pltpu.make_async_remote_copy(
            src_ref=ref, dst_ref=ref, send_sem=send_sem.at[k], recv_sem=recv_sem.at[k],
            device_id={"dp": peers[k]}, device_id_type=MESH,
        ).wait_recv()

    to_all(cnt.at[mine, :], cnt_send, cnt_recv)
    load_tok.wait()
    live = (tok[...] != 0).astype(F32)
    live_count = jnp.sum(live, axis=1, keepdims=True)

    pair.wait_recv()
    even, odd = pl.ds(0, half, stride=2), pl.ds(1, half, stride=2)
    out_even = (part[even, :] + other[even, :]) * live
    out_odd = (part[odd, :] + other[odd, :]) * live
    in_feat = part[rank:, :] + other[rank:, :]
    blank = jnp.zeros_like(in_feat)
    grads = lax.dot_general(
        jnp.concatenate([out_even, out_odd], axis=1),
        jnp.concatenate(
            [jnp.concatenate([in_feat, blank], axis=1), jnp.concatenate([blank, in_feat], axis=1)], axis=0
        ),
        NT,
        precision=lax.Precision.HIGHEST,
        preferred_element_type=F32,
    )
    feats[me] = (grads / live_count).astype(jnp.bfloat16)
    to_all(feats.at[me], feat_send, feat_recv)

    for k in range(n - 1):
        arrived(cnt.at[pl.ds(froms[k], 1), :], k, cnt_send, cnt_recv)
    row = lax.broadcasted_iota(jnp.int32, (boots, cnt.shape[1]), 0)
    col = lax.broadcasted_iota(jnp.int32, (boots, cnt.shape[1]), 1)
    pick = (col == row + me * boots).astype(F32)
    my_counts = lax.dot_general(
        pick, cnt[...].astype(F32), NT, precision=lax.Precision.HIGHEST, preferred_element_type=F32
    )

    def widen(source):
        rows = pl.ds(pl.multiple_of(source * half, half), half)
        wide[rows, :] = feats[source].astype(F32)

    widen(me)
    load_test.wait()
    for k in range(n - 1):
        arrived(feats.at[froms[k]], k, feat_send, feat_recv)
        widen(froms[k])
    flat = jnp.concatenate([wide[pl.ds(r, n, stride=half), :] for r in range(half)], axis=1)
    scores = lax.dot_general(flat.astype(jnp.bfloat16), test[...], NT, preferred_element_type=F32)

    def place(source):
        return pl.ds(pl.multiple_of(source * tests, tests), tests)

    every[:, place(me)] = scores
    to_all(every.at[:, place(me)], sc_send, sc_recv)
    for k in range(n - 1):
        arrived(every.at[:, place(froms[k])], k, sc_send, sc_recv)
    score_ref[...] = every[mine, :]
    boot_ref[...] = jnp.dot(my_counts, every[...], precision=lax.Precision.HIGHEST, preferred_element_type=F32)

    pair.wait_send()
    for copy in sends:
        copy.wait_send()


def fused(n, hidden_acts, out_grads, token_ids, proj_in, proj_out, test_feats, resample_counts):
    _, tokens, units = hidden_acts.shape
    rank, model = proj_out.shape
    tests = test_feats.shape[0]
    boots = resample_counts.shape[1]
    chunks = 4 if units % (4 * 128) == 0 else 1
    dma = pltpu.SemaphoreType.DMA
    any_spec = pl.BlockSpec(memory_space=pl.ANY)
    vmem = pl.BlockSpec(memory_space=pltpu.VMEM)
    return pl.pallas_call(
        functools.partial(kernel, n, chunks),
        out_shape=(
            jax.ShapeDtypeStruct((1, n * tests), F32),
            jax.ShapeDtypeStruct((boots // n, n * tests), F32),
        ),
        in_specs=[any_spec] * 7,
        out_specs=(vmem, vmem),
        scratch_shapes=[
            pltpu.VMEM((tokens, units), jnp.bfloat16),
            pltpu.VMEM((tokens, model), jnp.bfloat16),
            pltpu.VMEM((1, tokens), jnp.int32),
            pltpu.VMEM((rank, units), jnp.bfloat16),
            pltpu.VMEM((rank, model), jnp.bfloat16),
            pltpu.VMEM(test_feats.shape, jnp.bfloat16),
            pltpu.VMEM((n, boots), jnp.int32),
            pltpu.VMEM((2 * rank, tokens), F32),
            pltpu.VMEM((2 * rank, tokens), F32),
            pltpu.VMEM((n, rank // 2, 2 * rank), jnp.bfloat16),
            pltpu.VMEM((n * rank // 2, 2 * rank), F32),
            pltpu.VMEM((n, n * tests), F32),
            dma((5,)),
            dma((2, chunks)),
            dma((2,)),
        ] + [dma((n - 1,))] * 6,
        compiler_params=pltpu.CompilerParams(
            collective_id=0, has_side_effects=True, vmem_limit_bytes=32 * 1024 * 1024
        ),
        cost_estimate=pl.CostEstimate(flops=300_000_000, bytes_accessed=5_000_000, transcendentals=0),
    )(hidden_acts, out_grads, token_ids, proj_in, proj_out, test_feats, resample_counts)


def solution(mesh):
    n = mesh.shape["dp"]

    def body(*args):
        if args[0].shape[0] == 1 and args[5].shape[0] % 128 == 0:
            return fused(n, *args)
        return shards(*args)

    placed = (
        P(("groups", "dp"), None, "tensor"),
        P(("groups", "dp"), None, "tensor"),
        P(("groups", "dp"), None),
        P(None, "tensor"),
        P(None, "tensor"),
        P("dp", None),
        P(("groups", "dp"), None),
    )
    return jax.shard_map(
        body,
        mesh=mesh,
        in_specs=placed,
        out_specs=(P(("groups", "dp"), None), P(("groups", "dp"), None)),
        check_vma=False,
    )
```

```python
import functools

import jax
import jax.numpy as jnp
from jax import lax
from jax.experimental import pallas as pl
from jax.experimental.pallas import tpu as pltpu
from jax.sharding import PartitionSpec as P

MESH = pl.DeviceIdType.MESH
F32 = jnp.float32
NT = (((1,), (1,)), ((), ()))


def shards(hidden_acts, out_grads, token_ids, proj_in, proj_out, test_feats, resample_counts):
    token_live = (token_ids != 0).astype(jnp.float32)
    live_count = jnp.sum(token_live, axis=1)
    in_part = jnp.einsum("rf,elf->erl", proj_in, hidden_acts, preferred_element_type=jnp.float32)
    out_part = jnp.einsum("rd,eld->erl", proj_out, out_grads, preferred_element_type=jnp.float32)
    in_feat, out_feat = lax.psum((in_part, out_part), "tensor")
    example_grad = (
        jnp.einsum(
            "eol,eil->eoi",
            out_feat * token_live[:, None, :],
            in_feat,
            precision=lax.Precision.HIGHEST,
        )
        / live_count[:, None, None]
    )
    train_feats = example_grad.reshape(example_grad.shape[0], -1).astype(jnp.bfloat16)
    score_cols = lax.dot_general(
        lax.all_gather(train_feats, "dp", axis=0, tiled=True),
        test_feats,
        (((1,), (1,)), ((), ())),
        preferred_element_type=jnp.float32,
    )
    all_counts = lax.all_gather(resample_counts, "dp", axis=0, tiled=True).astype(jnp.float32)
    boot_cols = lax.dot_general(
        all_counts,
        score_cols,
        (((0,), (0,)), ((), ())),
        precision=lax.Precision.HIGHEST,
        preferred_element_type=jnp.float32,
    )
    score_local, boot_sums = (
        lax.all_to_all(score_cols, "dp", split_axis=0, concat_axis=1, tiled=True),
        lax.all_to_all(boot_cols, "dp", split_axis=0, concat_axis=1, tiled=True),
    )
    return (score_local, boot_sums)


def kernel(
    n, chunks,
    hid_hbm, grad_hbm, tok_hbm, pin_hbm, pout_hbm, test_hbm, cnt_hbm,
    score_ref, boot_ref,
    hid, grad, tok, pin, pout, test, cnt, part, other, feats, wide, every,
    load_sem, chunk_sem, pair_sem, cnt_send, cnt_recv, feat_send, feat_recv, sc_send, sc_recv,
):
    me = lax.axis_index("dp")
    core = lax.axis_index("tensor")
    rank = pout.shape[0]
    half = rank // 2
    tests = test.shape[0]
    boots = boot_ref.shape[0]
    peers = [lax.rem(me + k, n) for k in range(1, n)]
    froms = [lax.rem(me + n - k, n) for k in range(1, n)]

    barrier = pltpu.get_barrier_semaphore()
    pl.semaphore_signal(barrier, inc=1, device_id={"tensor": 1 - core}, device_id_type=MESH)
    for peer in peers:
        pl.semaphore_signal(barrier, inc=1, device_id={"dp": peer}, device_id_type=MESH)

    def load(src, dst, sem):
        copy = pltpu.make_async_copy(src, dst, sem)
        copy.start()
        return copy

    load_pout = load(pout_hbm, pout, load_sem.at[0])
    load_grad = load(grad_hbm.at[0], grad, load_sem.at[1])
    width = hid.shape[1] // chunks
    loads = []
    for c in range(chunks):
        cols = pl.ds(c * width, width)
        loads.append((
            load(pin_hbm.at[:, cols], pin.at[:, cols], chunk_sem.at[0, c]),
            load(hid_hbm.at[0, :, cols], hid.at[:, cols], chunk_sem.at[1, c]),
        ))
    mine = pl.ds(me, 1)
    load_cnt = load(cnt_hbm, cnt.at[mine, :], load_sem.at[2])
    load_tok = load(tok_hbm, tok, load_sem.at[3])
    load_test = load(test_hbm, test, load_sem.at[4])

    load_pout.wait()
    load_grad.wait()
    part[0:rank, :] = lax.dot_general(pout[...], grad[...], NT, preferred_element_type=F32)
    total = None
    for c in range(chunks):
        for copy in loads[c]:
            copy.wait()
        cols = slice(c * width, (c + 1) * width)
        term = lax.dot_general(pin[:, cols], hid[:, cols], NT, preferred_element_type=F32)
        total = term if total is None else total + term
    part[rank:, :] = total

    pl.semaphore_wait(barrier, n)
    pair = pltpu.make_async_remote_copy(
        src_ref=part, dst_ref=other, send_sem=pair_sem.at[0], recv_sem=pair_sem.at[1],
        device_id={"tensor": 1 - core}, device_id_type=MESH,
    )
    pair.start()

    load_cnt.wait()
    sends = []

    def to_all(ref, send_sem, recv_sem):
        for k, peer in enumerate(peers):
            copy = pltpu.make_async_remote_copy(
                src_ref=ref, dst_ref=ref, send_sem=send_sem.at[k], recv_sem=recv_sem.at[k],
                device_id={"dp": peer}, device_id_type=MESH,
            )
            copy.start()
            sends.append(copy)

    def arrived(ref, k, send_sem, recv_sem):
        pltpu.make_async_remote_copy(
            src_ref=ref, dst_ref=ref, send_sem=send_sem.at[k], recv_sem=recv_sem.at[k],
            device_id={"dp": peers[k]}, device_id_type=MESH,
        ).wait_recv()

    to_all(cnt.at[mine, :], cnt_send, cnt_recv)
    load_tok.wait()
    live = (tok[...] != 0).astype(F32)
    live_count = jnp.sum(live, axis=1, keepdims=True)

    pair.wait_recv()
    even, odd = pl.ds(0, half, stride=2), pl.ds(1, half, stride=2)
    out_even = (part[even, :] + other[even, :]) * live
    out_odd = (part[odd, :] + other[odd, :]) * live
    in_feat = part[rank:, :] + other[rank:, :]
    blank = jnp.zeros_like(in_feat)
    grads = lax.dot_general(
        jnp.concatenate([out_even, out_odd], axis=1),
        jnp.concatenate(
            [jnp.concatenate([in_feat, blank], axis=1), jnp.concatenate([blank, in_feat], axis=1)], axis=0
        ),
        NT,
        precision=lax.Precision.HIGHEST,
        preferred_element_type=F32,
    )
    feats[me] = (grads / live_count).astype(jnp.bfloat16)
    to_all(feats.at[me], feat_send, feat_recv)

    for k in range(n - 1):
        arrived(cnt.at[pl.ds(froms[k], 1), :], k, cnt_send, cnt_recv)
    row = lax.broadcasted_iota(jnp.int32, (boots, cnt.shape[1]), 0)
    col = lax.broadcasted_iota(jnp.int32, (boots, cnt.shape[1]), 1)
    pick = (col == row + me * boots).astype(F32)
    my_counts = lax.dot_general(
        pick, cnt[...].astype(F32), NT, precision=lax.Precision.HIGHEST, preferred_element_type=F32
    )

    def widen(source):
        rows = pl.ds(pl.multiple_of(source * half, half), half)
        wide[rows, :] = feats[source].astype(F32)

    widen(me)
    load_test.wait()
    for k in range(n - 1):
        arrived(feats.at[froms[k]], k, feat_send, feat_recv)
        widen(froms[k])
    flat = jnp.concatenate([wide[pl.ds(r, n, stride=half), :] for r in range(half)], axis=1)
    scores = lax.dot_general(flat.astype(jnp.bfloat16), test[...], NT, preferred_element_type=F32)

    def place(source):
        return pl.ds(pl.multiple_of(source * tests, tests), tests)

    every[:, place(me)] = scores
    to_all(every.at[:, place(me)], sc_send, sc_recv)
    for k in range(n - 1):
        arrived(every.at[:, place(froms[k])], k, sc_send, sc_recv)
    score_ref[...] = every[mine, :]
    boot_ref[...] = jnp.dot(my_counts, every[...], precision=lax.Precision.HIGHEST, preferred_element_type=F32)

    pair.wait_send()
    for copy in sends:
        copy.wait_send()


def fused(n, hidden_acts, out_grads, token_ids, proj_in, proj_out, test_feats, resample_counts):
    _, tokens, units = hidden_acts.shape
    rank, model = proj_out.shape
    tests = test_feats.shape[0]
    boots = resample_counts.shape[1]
    chunks = 4 if units % (4 * 128) == 0 else 1
    dma = pltpu.SemaphoreType.DMA
    in_hbm = pl.BlockSpec(memory_space=pl.ANY)
    vmem = pl.BlockSpec(memory_space=pltpu.VMEM)
    return pl.pallas_call(
        functools.partial(kernel, n, chunks),
        out_shape=(
            jax.ShapeDtypeStruct((1, n * tests), F32),
            jax.ShapeDtypeStruct((boots // n, n * tests), F32),
        ),
        in_specs=[in_hbm] * 7,
        out_specs=(vmem, vmem),
        scratch_shapes=[
            pltpu.VMEM((tokens, units), jnp.bfloat16),
            pltpu.VMEM((tokens, model), jnp.bfloat16),
            pltpu.VMEM((1, tokens), jnp.int32),
            pltpu.VMEM((rank, units), jnp.bfloat16),
            pltpu.VMEM((rank, model), jnp.bfloat16),
            pltpu.VMEM(test_feats.shape, jnp.bfloat16),
            pltpu.VMEM((n, boots), jnp.int32),
            pltpu.VMEM((2 * rank, tokens), F32),
            pltpu.VMEM((2 * rank, tokens), F32),
            pltpu.VMEM((n, rank // 2, 2 * rank), jnp.bfloat16),
            pltpu.VMEM((n * rank // 2, 2 * rank), F32),
            pltpu.VMEM((n, n * tests), F32),
            dma((5,)),
            dma((2, chunks)),
            dma((2,)),
        ] + [dma((n - 1,))] * 6,
        compiler_params=pltpu.CompilerParams(
            collective_id=0, has_side_effects=True, vmem_limit_bytes=60 * 1024 * 1024
        ),
        cost_estimate=pl.CostEstimate(flops=300_000_000, bytes_accessed=5_000_000, transcendentals=0),
    )(hidden_acts, out_grads, token_ids, proj_in, proj_out, test_feats, resample_counts)


def solution(mesh):
    n = mesh.shape["dp"]

    def body(*args):
        if args[0].shape[0] == 1 and args[5].shape[0] % 128 == 0:
            return fused(n, *args)
        return shards(*args)

    placed = (
        P(("groups", "dp"), None, "tensor"),
        P(("groups", "dp"), None, "tensor"),
        P(("groups", "dp"), None),
        P(None, "tensor"),
        P(None, "tensor"),
        P("dp", None),
        P(("groups", "dp"), None),
    )
    return jax.shard_map(
        body,
        mesh=mesh,
        in_specs=placed,
        out_specs=(P(("groups", "dp"), None), P(("groups", "dp"), None)),
        check_vma=False,
    )
```

```python
import functools

import jax
import jax.numpy as jnp
from jax import lax
from jax.experimental import pallas as pl
from jax.experimental.pallas import tpu as pltpu
from jax.sharding import PartitionSpec as P

MESH = pl.DeviceIdType.MESH
F32 = jnp.float32
NT = (((1,), (1,)), ((), ()))


def shards(hidden_acts, out_grads, token_ids, proj_in, proj_out, test_feats, resample_counts):
    token_live = (token_ids != 0).astype(jnp.float32)
    live_count = jnp.sum(token_live, axis=1)
    in_part = jnp.einsum("rf,elf->erl", proj_in, hidden_acts, preferred_element_type=jnp.float32)
    out_part = jnp.einsum("rd,eld->erl", proj_out, out_grads, preferred_element_type=jnp.float32)
    in_feat, out_feat = lax.psum((in_part, out_part), "tensor")
    example_grad = (
        jnp.einsum(
            "eol,eil->eoi",
            out_feat * token_live[:, None, :],
            in_feat,
            precision=lax.Precision.HIGHEST,
        )
        / live_count[:, None, None]
    )
    train_feats = example_grad.reshape(example_grad.shape[0], -1).astype(jnp.bfloat16)
    score_cols = lax.dot_general(
        lax.all_gather(train_feats, "dp", axis=0, tiled=True),
        test_feats,
        (((1,), (1,)), ((), ())),
        preferred_element_type=jnp.float32,
    )
    all_counts = lax.all_gather(resample_counts, "dp", axis=0, tiled=True).astype(jnp.float32)
    boot_cols = lax.dot_general(
        all_counts,
        score_cols,
        (((0,), (0,)), ((), ())),
        precision=lax.Precision.HIGHEST,
        preferred_element_type=jnp.float32,
    )
    score_local, boot_sums = (
        lax.all_to_all(score_cols, "dp", split_axis=0, concat_axis=1, tiled=True),
        lax.all_to_all(boot_cols, "dp", split_axis=0, concat_axis=1, tiled=True),
    )
    return (score_local, boot_sums)


def kernel(
    n, chunks,
    hid_hbm, grad_hbm, tok_hbm, pin_hbm, pout_hbm, test_hbm, cnt_hbm,
    score_ref, boot_ref,
    hid, grad, tok, pin, pout, test, cnt, part, other, feats, wide, every,
    load_sem, chunk_sem, pair_sem, cnt_send, cnt_recv, feat_send, feat_recv, sc_send, sc_recv,
):
    me = lax.axis_index("dp")
    core = lax.axis_index("tensor")
    rank = pout.shape[0]
    half = rank // 2
    tests = test.shape[0]
    boots = boot_ref.shape[0]
    peers = [lax.rem(me + k, n) for k in range(1, n)]
    froms = [lax.rem(me + n - k, n) for k in range(1, n)]

    barrier = pltpu.get_barrier_semaphore()
    pl.semaphore_signal(barrier, inc=1, device_id={"tensor": 1 - core}, device_id_type=MESH)
    for peer in peers:
        pl.semaphore_signal(barrier, inc=1, device_id={"dp": peer}, device_id_type=MESH)

    def load(src, dst, sem):
        copy = pltpu.make_async_copy(src, dst, sem)
        copy.start()
        return copy

    load_pout = load(pout_hbm, pout, load_sem.at[0])
    load_grad = load(grad_hbm.at[0], grad, load_sem.at[1])
    width = hid.shape[1] // chunks
    loads = []
    for c in range(chunks):
        cols = pl.ds(c * width, width)
        loads.append((
            load(pin_hbm.at[:, cols], pin.at[:, cols], chunk_sem.at[0, c]),
            load(hid_hbm.at[0, :, cols], hid.at[:, cols], chunk_sem.at[1, c]),
        ))
    mine = pl.ds(me, 1)
    load_cnt = load(cnt_hbm, cnt.at[mine, :], load_sem.at[2])
    load_tok = load(tok_hbm, tok, load_sem.at[3])
    load_test = load(test_hbm, test, load_sem.at[4])

    load_pout.wait()
    load_grad.wait()
    part[0:rank, :] = lax.dot_general(pout[...], grad[...], NT, preferred_element_type=F32)
    total = None
    for c in range(chunks):
        for copy in loads[c]:
            copy.wait()
        cols = slice(c * width, (c + 1) * width)
        term = lax.dot_general(pin[:, cols], hid[:, cols], NT, preferred_element_type=F32)
        total = term if total is None else total + term
    part[rank:, :] = total

    pl.semaphore_wait(barrier, n)
    pair = pltpu.make_async_remote_copy(
        src_ref=part, dst_ref=other, send_sem=pair_sem.at[0], recv_sem=pair_sem.at[1],
        device_id={"tensor": 1 - core}, device_id_type=MESH,
    )
    pair.start()

    load_cnt.wait()
    sends = []

    def to_all(ref, send_sem, recv_sem):
        for k, peer in enumerate(peers):
            copy = pltpu.make_async_remote_copy(
                src_ref=ref, dst_ref=ref, send_sem=send_sem.at[k], recv_sem=recv_sem.at[k],
                device_id={"dp": peer}, device_id_type=MESH,
            )
            copy.start()
            sends.append(copy)

    def arrived(ref, k, send_sem, recv_sem):
        pltpu.make_async_remote_copy(
            src_ref=ref, dst_ref=ref, send_sem=send_sem.at[k], recv_sem=recv_sem.at[k],
            device_id={"dp": peers[k]}, device_id_type=MESH,
        ).wait_recv()

    to_all(cnt.at[mine, :], cnt_send, cnt_recv)
    load_tok.wait()
    live = (tok[...] != 0).astype(F32)
    live_count = jnp.sum(live, axis=1, keepdims=True)

    pair.wait_recv()
    even, odd = pl.ds(0, half, stride=2), pl.ds(1, half, stride=2)
    out_even = (part[even, :] + other[even, :]) * live
    out_odd = (part[odd, :] + other[odd, :]) * live
    in_feat = part[rank:, :] + other[rank:, :]
    blank = jnp.zeros_like(in_feat)
    grads = lax.dot_general(
        jnp.concatenate([out_even, out_odd], axis=1),
        jnp.concatenate(
            [jnp.concatenate([in_feat, blank], axis=1), jnp.concatenate([blank, in_feat], axis=1)], axis=0
        ),
        NT,
        precision=lax.Precision.HIGHEST,
        preferred_element_type=F32,
    )
    feats[me] = (grads / live_count).astype(jnp.bfloat16)
    to_all(feats.at[me], feat_send, feat_recv)

    for k in range(n - 1):
        arrived(cnt.at[pl.ds(froms[k], 1), :], k, cnt_send, cnt_recv)
    row = lax.broadcasted_iota(jnp.int32, (boots, cnt.shape[1]), 0)
    col = lax.broadcasted_iota(jnp.int32, (boots, cnt.shape[1]), 1)
    pick = (col == row + me * boots).astype(F32)
    my_counts = lax.dot_general(
        pick, cnt[...].astype(F32), NT, precision=lax.Precision.HIGHEST, preferred_element_type=F32
    )

    def widen(source):
        rows = pl.ds(pl.multiple_of(source * half, half), half)
        wide[rows, :] = feats[source].astype(F32)

    widen(me)
    load_test.wait()
    for k in range(n - 1):
        arrived(feats.at[froms[k]], k, feat_send, feat_recv)
        widen(froms[k])
    flat = jnp.concatenate([wide[pl.ds(r, n, stride=half), :] for r in range(half)], axis=1)
    scores = lax.dot_general(flat.astype(jnp.bfloat16), test[...], NT, preferred_element_type=F32)

    def place(source):
        return pl.ds(pl.multiple_of(source * tests, tests), tests)

    every[:, place(me)] = scores
    to_all(every.at[:, place(me)], sc_send, sc_recv)
    for k in range(n - 1):
        arrived(every.at[:, place(froms[k])], k, sc_send, sc_recv)
    score_ref[...] = every[mine, :]
    boot_ref[...] = jnp.dot(my_counts, every[...], precision=lax.Precision.HIGHEST, preferred_element_type=F32)

    pair.wait_send()
    for copy in sends:
        copy.wait_send()


def fused(n, *operands):
    hidden_acts, _, _, _, proj_out, test_feats, resample_counts = operands
    _, tokens, units = hidden_acts.shape
    rank, model = proj_out.shape
    tests = test_feats.shape[0]
    boots = resample_counts.shape[1]
    chunks = 4 if units % (4 * 128) == 0 else 1
    dma = pltpu.SemaphoreType.DMA
    in_hbm = pl.BlockSpec(memory_space=pl.ANY)
    vmem = pl.BlockSpec(memory_space=pltpu.VMEM)
    return pl.pallas_call(
        functools.partial(kernel, n, chunks),
        out_shape=(
            jax.ShapeDtypeStruct((1, n * tests), F32),
            jax.ShapeDtypeStruct((boots // n, n * tests), F32),
        ),
        in_specs=[in_hbm] * 7,
        out_specs=(vmem, vmem),
        scratch_shapes=[
            pltpu.VMEM((tokens, units), jnp.bfloat16),
            pltpu.VMEM((tokens, model), jnp.bfloat16),
            pltpu.VMEM((1, tokens), jnp.int32),
            pltpu.VMEM((rank, units), jnp.bfloat16),
            pltpu.VMEM((rank, model), jnp.bfloat16),
            pltpu.VMEM(test_feats.shape, jnp.bfloat16),
            pltpu.VMEM((n, boots), jnp.int32),
            pltpu.VMEM((2 * rank, tokens), F32),
            pltpu.VMEM((2 * rank, tokens), F32),
            pltpu.VMEM((n, rank // 2, 2 * rank), jnp.bfloat16),
            pltpu.VMEM((n * rank // 2, 2 * rank), F32),
            pltpu.VMEM((n, n * tests), F32),
            dma((5,)),
            dma((2, chunks)),
            dma((2,)),
        ] + [dma((n - 1,))] * 6,
        compiler_params=pltpu.CompilerParams(
            collective_id=0, has_side_effects=True, vmem_limit_bytes=32 * 1024 * 1024
        ),
        cost_estimate=pl.CostEstimate(flops=300_000_000, bytes_accessed=5_000_000, transcendentals=0),
    )(*[pltpu.with_memory_space_constraint(x, pltpu.HBM) for x in operands])


def solution(mesh):
    n = mesh.shape["dp"]

    def body(*args):
        if args[0].shape[0] == 1 and args[5].shape[0] % 128 == 0:
            return fused(n, *args)
        return shards(*args)

    placed = (
        P(("groups", "dp"), None, "tensor"),
        P(("groups", "dp"), None, "tensor"),
        P(("groups", "dp"), None),
        P(None, "tensor"),
        P(None, "tensor"),
        P("dp", None),
        P(("groups", "dp"), None),
    )
    return jax.shard_map(
        body,
        mesh=mesh,
        in_specs=placed,
        out_specs=(P(("groups", "dp"), None), P(("groups", "dp"), None)),
        check_vma=False,
    )
```

```python
import functools

import jax
import jax.numpy as jnp
from jax import lax
from jax.experimental import pallas as pl
from jax.experimental.pallas import tpu as pltpu
from jax.sharding import PartitionSpec as P

MESH = pl.DeviceIdType.MESH
F32 = jnp.float32
NT = (((1,), (1,)), ((), ()))


def shards(hidden_acts, out_grads, token_ids, proj_in, proj_out, test_feats, resample_counts):
    token_live = (token_ids != 0).astype(jnp.float32)
    live_count = jnp.sum(token_live, axis=1)
    in_part = jnp.einsum("rf,elf->erl", proj_in, hidden_acts, preferred_element_type=jnp.float32)
    out_part = jnp.einsum("rd,eld->erl", proj_out, out_grads, preferred_element_type=jnp.float32)
    in_feat, out_feat = lax.psum((in_part, out_part), "tensor")
    example_grad = (
        jnp.einsum(
            "eol,eil->eoi",
            out_feat * token_live[:, None, :],
            in_feat,
            precision=lax.Precision.HIGHEST,
        )
        / live_count[:, None, None]
    )
    train_feats = example_grad.reshape(example_grad.shape[0], -1).astype(jnp.bfloat16)
    score_cols = lax.dot_general(
        lax.all_gather(train_feats, "dp", axis=0, tiled=True),
        test_feats,
        (((1,), (1,)), ((), ())),
        preferred_element_type=jnp.float32,
    )
    all_counts = lax.all_gather(resample_counts, "dp", axis=0, tiled=True).astype(jnp.float32)
    boot_cols = lax.dot_general(
        all_counts,
        score_cols,
        (((0,), (0,)), ((), ())),
        precision=lax.Precision.HIGHEST,
        preferred_element_type=jnp.float32,
    )
    score_local, boot_sums = (
        lax.all_to_all(score_cols, "dp", split_axis=0, concat_axis=1, tiled=True),
        lax.all_to_all(boot_cols, "dp", split_axis=0, concat_axis=1, tiled=True),
    )
    return (score_local, boot_sums)


def partners(me, n):
    if n & (n - 1):
        return [lax.rem(me + k, n) for k in range(1, n)], [lax.rem(me + n - k, n) for k in range(1, n)]
    peers = []
    for k in range(n - 1, 0, -1):
        peer, bit = me, 1
        while bit < n:
            if k & bit:
                peer = peer + bit * (1 - 2 * lax.rem(me // bit, 2))
            bit *= 2
        peers.append(peer)
    return peers, peers


def kernel(
    n, chunks,
    hid_hbm, grad_hbm, tok_hbm, pin_hbm, pout_hbm, test_hbm, cnt_hbm,
    score_ref, boot_ref,
    hid, grad, tok, pin, pout, test, cnt, part, other, feats, wide, every,
    load_sem, chunk_sem, pair_sem, cnt_send, cnt_recv, feat_send, feat_recv, sc_send, sc_recv,
):
    me = lax.axis_index("dp")
    core = lax.axis_index("tensor")
    rank = pout.shape[0]
    half = rank // 2
    tests = test.shape[0]
    boots = boot_ref.shape[0]
    peers, froms = partners(me, n)

    def load(src, dst, sem):
        copy = pltpu.make_async_copy(src, dst, sem)
        copy.start()
        return copy

    load_pout = load(pout_hbm, pout, load_sem.at[0])
    load_grad = load(grad_hbm.at[0], grad, load_sem.at[1])
    width = hid.shape[1] // chunks
    loads = []
    for c in range(chunks):
        cols = pl.ds(c * width, width)
        loads.append((
            load(pin_hbm.at[:, cols], pin.at[:, cols], chunk_sem.at[0, c]),
            load(hid_hbm.at[0, :, cols], hid.at[:, cols], chunk_sem.at[1, c]),
        ))
    mine = pl.ds(me, 1)
    load_cnt = load(cnt_hbm, cnt.at[mine, :], load_sem.at[2])
    load_tok = load(tok_hbm, tok, load_sem.at[3])

    barrier = pltpu.get_barrier_semaphore()
    pl.semaphore_signal(barrier, inc=1, device_id={"tensor": 1 - core}, device_id_type=MESH)
    for peer in peers:
        pl.semaphore_signal(barrier, inc=1, device_id={"dp": peer}, device_id_type=MESH)

    load_pout.wait()
    load_grad.wait()
    part[0:rank, :] = lax.dot_general(pout[...], grad[...], NT, preferred_element_type=F32)
    total = None
    for c in range(chunks):
        for copy in loads[c]:
            copy.wait()
        cols = slice(c * width, (c + 1) * width)
        term = lax.dot_general(pin[:, cols], hid[:, cols], NT, preferred_element_type=F32)
        total = term if total is None else total + term
    load_test = load(test_hbm, test, load_sem.at[4])
    part[rank:, :] = total

    pl.semaphore_wait(barrier, n)
    pair = pltpu.make_async_remote_copy(
        src_ref=part, dst_ref=other, send_sem=pair_sem.at[0], recv_sem=pair_sem.at[1],
        device_id={"tensor": 1 - core}, device_id_type=MESH,
    )
    pair.start()

    load_cnt.wait()
    sends = []

    def to_all(ref, send_sem, recv_sem):
        for k, peer in enumerate(peers):
            copy = pltpu.make_async_remote_copy(
                src_ref=ref, dst_ref=ref, send_sem=send_sem.at[k], recv_sem=recv_sem.at[k],
                device_id={"dp": peer}, device_id_type=MESH,
            )
            copy.start()
            sends.append(copy)

    def arrived(ref, k, send_sem, recv_sem):
        pltpu.make_async_remote_copy(
            src_ref=ref, dst_ref=ref, send_sem=send_sem.at[k], recv_sem=recv_sem.at[k],
            device_id={"dp": peers[k]}, device_id_type=MESH,
        ).wait_recv()

    load_tok.wait()
    live = (tok[...] != 0).astype(F32)
    live_count = jnp.sum(live, axis=1, keepdims=True)

    pair.wait_recv()
    even, odd = pl.ds(0, half, stride=2), pl.ds(1, half, stride=2)
    out_even = (part[even, :] + other[even, :]) * live
    out_odd = (part[odd, :] + other[odd, :]) * live
    in_feat = part[rank:, :] + other[rank:, :]
    blank = jnp.zeros_like(in_feat)
    grads = lax.dot_general(
        jnp.concatenate([out_even, out_odd], axis=1),
        jnp.concatenate(
            [jnp.concatenate([in_feat, blank], axis=1), jnp.concatenate([blank, in_feat], axis=1)], axis=0
        ),
        NT,
        precision=lax.Precision.HIGHEST,
        preferred_element_type=F32,
    )
    feats[me] = (grads / live_count).astype(jnp.bfloat16)
    to_all(feats.at[me], feat_send, feat_recv)
    to_all(cnt.at[mine, :], cnt_send, cnt_recv)

    def widen(source):
        rows = pl.ds(pl.multiple_of(source * half, half), half)
        wide[rows, :] = feats[source].astype(F32)

    widen(me)
    load_test.wait()
    for k in range(n - 1):
        arrived(feats.at[froms[k]], k, feat_send, feat_recv)
        widen(froms[k])
    flat = jnp.concatenate([wide[pl.ds(r, n, stride=half), :] for r in range(half)], axis=1)
    scores = lax.dot_general(flat.astype(jnp.bfloat16), test[...], NT, preferred_element_type=F32)

    def place(source):
        return pl.ds(pl.multiple_of(source * tests, tests), tests)

    every[:, place(me)] = scores
    to_all(every.at[:, place(me)], sc_send, sc_recv)

    for k in range(n - 1):
        arrived(cnt.at[pl.ds(froms[k], 1), :], k, cnt_send, cnt_recv)
    row = lax.broadcasted_iota(jnp.int32, (boots, cnt.shape[1]), 0)
    col = lax.broadcasted_iota(jnp.int32, (boots, cnt.shape[1]), 1)
    pick = (col == row + me * boots).astype(F32)
    my_counts = lax.dot_general(
        pick, cnt[...].astype(F32), NT, precision=lax.Precision.HIGHEST, preferred_element_type=F32
    )
    for k in range(n - 1):
        arrived(every.at[:, place(froms[k])], k, sc_send, sc_recv)
    score_ref[...] = every[mine, :]
    sums = my_counts[:, 0:1] * every[0:1, :]
    for e in range(1, n):
        sums = sums + my_counts[:, e:e + 1] * every[e:e + 1, :]
    boot_ref[...] = sums

    pair.wait_send()
    for copy in sends:
        copy.wait_send()


def fused(n, *operands):
    hidden_acts, _, _, _, proj_out, test_feats, resample_counts = operands
    _, tokens, units = hidden_acts.shape
    rank, model = proj_out.shape
    tests = test_feats.shape[0]
    boots = resample_counts.shape[1]
    chunks = 2 if units % (2 * 128) == 0 else 1
    dma = pltpu.SemaphoreType.DMA
    in_hbm = pl.BlockSpec(memory_space=pl.ANY)
    vmem = pl.BlockSpec(memory_space=pltpu.VMEM)
    return pl.pallas_call(
        functools.partial(kernel, n, chunks),
        out_shape=(
            jax.ShapeDtypeStruct((1, n * tests), F32),
            jax.ShapeDtypeStruct((boots // n, n * tests), F32),
        ),
        in_specs=[in_hbm] * 7,
        out_specs=(vmem, vmem),
        scratch_shapes=[
            pltpu.VMEM((tokens, units), jnp.bfloat16),
            pltpu.VMEM((tokens, model), jnp.bfloat16),
            pltpu.VMEM((1, tokens), jnp.int32),
            pltpu.VMEM((rank, units), jnp.bfloat16),
            pltpu.VMEM((rank, model), jnp.bfloat16),
            pltpu.VMEM(test_feats.shape, jnp.bfloat16),
            pltpu.VMEM((n, boots), jnp.int32),
            pltpu.VMEM((2 * rank, tokens), F32),
            pltpu.VMEM((2 * rank, tokens), F32),
            pltpu.VMEM((n, rank // 2, 2 * rank), jnp.bfloat16),
            pltpu.VMEM((n * rank // 2, 2 * rank), F32),
            pltpu.VMEM((n, n * tests), F32),
            dma((5,)),
            dma((2, chunks)),
            dma((2,)),
        ] + [dma((n - 1,))] * 6,
        compiler_params=pltpu.CompilerParams(
            collective_id=0, has_side_effects=True, vmem_limit_bytes=32 * 1024 * 1024
        ),
        cost_estimate=pl.CostEstimate(flops=300_000_000, bytes_accessed=5_000_000, transcendentals=0),
    )(*[pltpu.with_memory_space_constraint(x, pltpu.HBM) for x in operands])


def solution(mesh):
    n = mesh.shape["dp"]

    def body(*args):
        if args[0].shape[0] == 1 and args[5].shape[0] % 128 == 0:
            return fused(n, *args)
        return shards(*args)

    placed = (
        P(("groups", "dp"), None, "tensor"),
        P(("groups", "dp"), None, "tensor"),
        P(("groups", "dp"), None),
        P(None, "tensor"),
        P(None, "tensor"),
        P("dp", None),
        P(("groups", "dp"), None),
    )
    return jax.shard_map(
        body,
        mesh=mesh,
        in_specs=placed,
        out_specs=(P(("groups", "dp"), None), P(("groups", "dp"), None)),
        check_vma=False,
    )
```

```python
import functools

import jax
import jax.numpy as jnp
from jax import lax
from jax.experimental import pallas as pl
from jax.experimental.pallas import tpu as pltpu
from jax.sharding import PartitionSpec as P

MESH = pl.DeviceIdType.MESH
F32 = jnp.float32
NT = (((1,), (1,)), ((), ()))


def shards(hidden_acts, out_grads, token_ids, proj_in, proj_out, test_feats, resample_counts):
    token_live = (token_ids != 0).astype(jnp.float32)
    live_count = jnp.sum(token_live, axis=1)
    in_part = jnp.einsum("rf,elf->erl", proj_in, hidden_acts, preferred_element_type=jnp.float32)
    out_part = jnp.einsum("rd,eld->erl", proj_out, out_grads, preferred_element_type=jnp.float32)
    in_feat, out_feat = lax.psum((in_part, out_part), "tensor")
    example_grad = (
        jnp.einsum(
            "eol,eil->eoi",
            out_feat * token_live[:, None, :],
            in_feat,
            precision=lax.Precision.HIGHEST,
        )
        / live_count[:, None, None]
    )
    train_feats = example_grad.reshape(example_grad.shape[0], -1).astype(jnp.bfloat16)
    score_cols = lax.dot_general(
        lax.all_gather(train_feats, "dp", axis=0, tiled=True),
        test_feats,
        (((1,), (1,)), ((), ())),
        preferred_element_type=jnp.float32,
    )
    all_counts = lax.all_gather(resample_counts, "dp", axis=0, tiled=True).astype(jnp.float32)
    boot_cols = lax.dot_general(
        all_counts,
        score_cols,
        (((0,), (0,)), ((), ())),
        precision=lax.Precision.HIGHEST,
        preferred_element_type=jnp.float32,
    )
    score_local, boot_sums = (
        lax.all_to_all(score_cols, "dp", split_axis=0, concat_axis=1, tiled=True),
        lax.all_to_all(boot_cols, "dp", split_axis=0, concat_axis=1, tiled=True),
    )
    return (score_local, boot_sums)


def partners(me, n):
    if n & (n - 1):
        return [lax.rem(me + k, n) for k in range(1, n)], [lax.rem(me + n - k, n) for k in range(1, n)]
    peers = []
    for k in range(n - 1, 0, -1):
        peer, bit = me, 1
        while bit < n:
            if k & bit:
                peer = peer + bit * (1 - 2 * lax.rem(me // bit, 2))
            bit *= 2
        peers.append(peer)
    return peers, peers


def kernel(
    n, chunks,
    hid_hbm, grad_hbm, tok_hbm, pin_hbm, pout_hbm, test_hbm, cnt_hbm,
    score_ref, boot_ref,
    hid, grad, tok, pin, pout, test, cnt, part, other, feats, wide, every,
    load_sem, chunk_sem, pair_sem, cnt_send, cnt_recv, feat_send, feat_recv, sc_send, sc_recv,
):
    me = lax.axis_index("dp")
    core = lax.axis_index("tensor")
    rank = pout.shape[0]
    half = rank // 2
    tests = test.shape[0]
    boots = boot_ref.shape[0]
    peers, froms = partners(me, n)

    def load(src, dst, sem):
        copy = pltpu.make_async_copy(src, dst, sem)
        copy.start()
        return copy

    load_pout = load(pout_hbm, pout, load_sem.at[0])
    load_grad = load(grad_hbm.at[0], grad, load_sem.at[1])
    width = hid.shape[1] // chunks
    loads = []
    for c in range(chunks):
        cols = pl.ds(c * width, width)
        loads.append((
            load(pin_hbm.at[:, cols], pin.at[:, cols], chunk_sem.at[0, c]),
            load(hid_hbm.at[0, :, cols], hid.at[:, cols], chunk_sem.at[1, c]),
        ))
    mine = pl.ds(me, 1)
    load_cnt = load(cnt_hbm, cnt.at[mine, :], load_sem.at[2])
    load_tok = load(tok_hbm, tok, load_sem.at[3])

    barrier = pltpu.get_barrier_semaphore()
    pl.semaphore_signal(barrier, inc=1, device_id={"tensor": 1 - core}, device_id_type=MESH)
    for peer in peers:
        pl.semaphore_signal(barrier, inc=1, device_id={"dp": peer}, device_id_type=MESH)

    load_pout.wait()
    load_grad.wait()
    part[0:rank, :] = lax.dot_general(pout[...], grad[...], NT, preferred_element_type=F32)
    total = None
    for c in range(chunks):
        for copy in loads[c]:
            copy.wait()
        cols = slice(c * width, (c + 1) * width)
        term = lax.dot_general(pin[:, cols], hid[:, cols], NT, preferred_element_type=F32)
        total = term if total is None else total + term
    load_test = load(test_hbm, test, load_sem.at[4])
    part[rank:, :] = total

    pl.semaphore_wait(barrier, n)
    pair = pltpu.make_async_remote_copy(
        src_ref=part, dst_ref=other, send_sem=pair_sem.at[0], recv_sem=pair_sem.at[1],
        device_id={"tensor": 1 - core}, device_id_type=MESH,
    )
    pair.start()

    load_cnt.wait()
    sends = []

    def to_all(ref, send_sem, recv_sem):
        for k, peer in enumerate(peers):
            copy = pltpu.make_async_remote_copy(
                src_ref=ref, dst_ref=ref, send_sem=send_sem.at[k], recv_sem=recv_sem.at[k],
                device_id={"dp": peer}, device_id_type=MESH,
            )
            copy.start()
            sends.append(copy)

    def arrived(ref, k, send_sem, recv_sem):
        pltpu.make_async_remote_copy(
            src_ref=ref, dst_ref=ref, send_sem=send_sem.at[k], recv_sem=recv_sem.at[k],
            device_id={"dp": peers[k]}, device_id_type=MESH,
        ).wait_recv()

    load_tok.wait()
    live = (tok[...] != 0).astype(F32)
    live_count = jnp.sum(live, axis=1, keepdims=True)

    pair.wait_recv()
    even, odd = pl.ds(0, half, stride=2), pl.ds(1, half, stride=2)
    out_even = (part[even, :] + other[even, :]) * live
    out_odd = (part[odd, :] + other[odd, :]) * live
    in_feat = part[rank:, :] + other[rank:, :]
    both = lax.dot_general(
        jnp.concatenate([out_even, out_odd], axis=0),
        in_feat,
        NT,
        precision=lax.Precision.HIGHEST,
        preferred_element_type=F32,
    )
    grads = jnp.concatenate([both[:half], both[half:]], axis=1)
    feats[me] = (grads / live_count).astype(jnp.bfloat16)
    to_all(feats.at[me], feat_send, feat_recv)
    to_all(cnt.at[mine, :], cnt_send, cnt_recv)

    def widen(source):
        rows = pl.ds(pl.multiple_of(source * half, half), half)
        wide[rows, :] = feats[source].astype(F32)

    widen(me)
    load_test.wait()
    for k in range(n - 1):
        arrived(feats.at[froms[k]], k, feat_send, feat_recv)
        widen(froms[k])
    flat = jnp.concatenate([wide[pl.ds(r, n, stride=half), :] for r in range(half)], axis=1)
    scores = lax.dot_general(flat.astype(jnp.bfloat16), test[...], NT, preferred_element_type=F32)

    def place(source):
        return pl.ds(pl.multiple_of(source * tests, tests), tests)

    every[:, place(me)] = scores
    to_all(every.at[:, place(me)], sc_send, sc_recv)

    for k in range(n - 1):
        arrived(cnt.at[pl.ds(froms[k], 1), :], k, cnt_send, cnt_recv)
    row = lax.broadcasted_iota(jnp.int32, (boots, cnt.shape[1]), 0)
    col = lax.broadcasted_iota(jnp.int32, (boots, cnt.shape[1]), 1)
    pick = (col == row + me * boots).astype(F32)
    my_counts = lax.dot_general(
        pick, cnt[...].astype(F32), NT, precision=lax.Precision.HIGHEST, preferred_element_type=F32
    )
    for k in range(n - 1):
        arrived(every.at[:, place(froms[k])], k, sc_send, sc_recv)
    score_ref[...] = every[mine, :]
    sums = my_counts[:, 0:1] * every[0:1, :]
    for e in range(1, n):
        sums = sums + my_counts[:, e:e + 1] * every[e:e + 1, :]
    boot_ref[...] = sums

    pair.wait_send()
    for copy in sends:
        copy.wait_send()


def fused(n, *operands):
    hidden_acts, _, _, _, proj_out, test_feats, resample_counts = operands
    _, tokens, units = hidden_acts.shape
    rank, model = proj_out.shape
    tests = test_feats.shape[0]
    boots = resample_counts.shape[1]
    chunks = 2 if units % (2 * 128) == 0 else 1
    dma = pltpu.SemaphoreType.DMA
    in_hbm = pl.BlockSpec(memory_space=pl.ANY)
    vmem = pl.BlockSpec(memory_space=pltpu.VMEM)
    return pl.pallas_call(
        functools.partial(kernel, n, chunks),
        out_shape=(
            jax.ShapeDtypeStruct((1, n * tests), F32),
            jax.ShapeDtypeStruct((boots // n, n * tests), F32),
        ),
        in_specs=[in_hbm] * 7,
        out_specs=(vmem, vmem),
        scratch_shapes=[
            pltpu.VMEM((tokens, units), jnp.bfloat16),
            pltpu.VMEM((tokens, model), jnp.bfloat16),
            pltpu.VMEM((1, tokens), jnp.int32),
            pltpu.VMEM((rank, units), jnp.bfloat16),
            pltpu.VMEM((rank, model), jnp.bfloat16),
            pltpu.VMEM(test_feats.shape, jnp.bfloat16),
            pltpu.VMEM((n, boots), jnp.int32),
            pltpu.VMEM((2 * rank, tokens), F32),
            pltpu.VMEM((2 * rank, tokens), F32),
            pltpu.VMEM((n, rank // 2, 2 * rank), jnp.bfloat16),
            pltpu.VMEM((n * rank // 2, 2 * rank), F32),
            pltpu.VMEM((n, n * tests), F32),
            dma((5,)),
            dma((2, chunks)),
            dma((2,)),
        ] + [dma((n - 1,))] * 6,
        compiler_params=pltpu.CompilerParams(
            collective_id=0, has_side_effects=True, vmem_limit_bytes=32 * 1024 * 1024
        ),
        cost_estimate=pl.CostEstimate(flops=300_000_000, bytes_accessed=5_000_000, transcendentals=0),
    )(*[pltpu.with_memory_space_constraint(x, pltpu.HBM) for x in operands])


def solution(mesh):
    n = mesh.shape["dp"]

    def body(*args):
        if args[0].shape[0] == 1 and args[5].shape[0] % 128 == 0:
            return fused(n, *args)
        return shards(*args)

    placed = (
        P(("groups", "dp"), None, "tensor"),
        P(("groups", "dp"), None, "tensor"),
        P(("groups", "dp"), None),
        P(None, "tensor"),
        P(None, "tensor"),
        P("dp", None),
        P(("groups", "dp"), None),
    )
    return jax.shard_map(
        body,
        mesh=mesh,
        in_specs=placed,
        out_specs=(P(("groups", "dp"), None), P(("groups", "dp"), None)),
        check_vma=False,
    )
```
